32 devices in a mesh: win: 2 (over x), chan: 4 (over y, core), tm: 4 (over z).
Axes of the slice: x: 2, y: 2, z: 4, core: 2. Of those that a mesh axis runs over, the one named last changes fastest.
Arguments:
- samples: bfloat16 [256, 65536], P(('win', 'chan'), 'tm'), parts along dimension 0, may hold values from -6 to 6
- gap_start: int32 [256, 4], P(('win', 'chan')), parts along dimension 0, may hold values from 0 to 255, as said below
- gap_len: int32 [256, 4], P(('win', 'chan')), parts along dimension 0, may hold values from 0 to 16, as said below
- offsets: int32 [32], replicated, may hold values from -32 to 32, as said below
Outputs:
- correlation: float32 [32, 256, 1024], P('tm', ('win', 'chan')), parts along dimension 1
The draws below stay inside these ranges and needn't reach their ends.
There are 2 independent parts, one for each index of `win`. The reference program is written for one: setup_inputs(seed, part) draws one part's arguments, and reference() takes and returns one part's arrays. A program takes and returns all parts, laid end to end along the dimension named above; an argument that names none is the same for every part. Nothing has to cross between parts.
Inputs may be any that keep to these rules, and one draw needn't show every extreme that they name: `gap_start`: A gap may intersection others and run past the window's end. `gap_len`: A length of 0 is no gap; some channels carry far longer gaps than others. 32 distinct nonzero offsets; both -32 and 32 are among them.
All inputs are finite; a program needn't handle non-finite values.
Results may differ from the reference program's by a relative error of at most 0.0056.
Values may be sent and summed in bfloat16 or wider, within the bound.
A program may use at most 128 MiB of HBM per device.

```python
import math
import jax
import jax.numpy as jnp
from jax import lax

CH_DEV = 32
NFFT = 2048
LAGS = 1024
NB = 32
R = 32
BAND = 64
BLK = 256
GAPS = 4
MAXGAP = 16
NF = 1024
HOP = 1024
NT = 65536
NBLK = 256
SEGMENTS = 64
CHANNELS = 128


def draw_gap_start(key, part):
    starts = jax.random.randint(jax.random.fold_in(key, 11), (CHANNELS, GAPS), 0, NBLK)
    chosen = jax.random.randint(jax.random.fold_in(key, 12), (), 0, CHANNELS)
    rows = jnp.arange(CHANNELS, dtype=jnp.int32)[:, None]
    cols = jnp.arange(GAPS, dtype=jnp.int32)[None, :]
    return jnp.where((rows == chosen) & (cols == 0), NBLK - 1, starts).astype(jnp.int32)


def draw_gap_len(key, part):
    heavy = jax.random.randint(jax.random.fold_in(key, 21), (CHANNELS, 1), 0, 4) == 0
    lengths = jax.random.randint(jax.random.fold_in(key, 22), (CHANNELS, GAPS), 0, MAXGAP + 1)
    lengths = jnp.where(heavy, lengths, lengths // 4)
    chosen = jax.random.randint(jax.random.fold_in(key, 23), (), 0, CHANNELS)
    rows = jnp.arange(CHANNELS, dtype=jnp.int32)[:, None]
    cols = jnp.arange(GAPS, dtype=jnp.int32)[None, :]
    return jnp.where((rows == chosen) & (cols == 0), MAXGAP, lengths).astype(jnp.int32)


def draw_offsets(key, part):
    values = jnp.arange(2 * R, dtype=jnp.int32)
    places = jax.random.permutation(jax.random.fold_in(key, 31), 2 * R).astype(jnp.int32)
    places = jnp.where(values == 0, -2, jnp.where(values == 2 * R - 1, -1, places))
    picked = jnp.argsort(places, stable=True)[:NB].astype(jnp.int32)
    picked = jax.random.permutation(jax.random.fold_in(key, 32), picked).astype(jnp.int32)
    return jnp.where(picked < R, picked - R, picked - R + 1).astype(jnp.int32)


def level_of(own_key, dims, shards, least, high):
    def one(dim, shards_of):
        steps = jax.random.uniform(jax.random.fold_in(jax.random.fold_in(own_key, 6), dim), (shards_of,), jnp.float32, least / len(shards), high / len(shards))
        return jnp.repeat(jnp.exp(steps), dims[dim] // shards_of).reshape((-1,) + (1,) * (len(dims) - dim - 1))

    gain = one(*shards[0])
    for cut in shards[1:]:
        gain = gain * one(*cut)
    return gain


def noise(key, dims, scale, limit, shards=(), kind=jnp.bfloat16):
    array = jax.random.normal(key, dims, jnp.float32) * scale
    if len(shards) > 0:
        array = level_of(key, dims, shards, -0.22, 0.18) * array
    return jnp.clip(array, min=-limit, max=limit).astype(kind)


def setup_inputs(seed: int = 0, part: int = 0) -> dict:
    splits = jax.random.split(jax.random.key(seed), 5)
    part_keys = jax.random.split(jax.random.fold_in(splits[4], part), 5)
    return {
        "samples": noise(part_keys[0], (CHANNELS, NT), 1.0, 6.0, ((0, 4), (1, 4))),
        "gap_start": draw_gap_start(jax.random.fold_in(jax.random.fold_in(splits[4], part), 71), part),
        "gap_len": draw_gap_len(jax.random.fold_in(jax.random.fold_in(splits[4], part), 71), part),
        "offsets": draw_offsets(jax.random.fold_in(splits[4], 71), part),
    }


def dft_table():
    rows = jnp.arange(NFFT, dtype=jnp.int32)[:, None]
    freqs = jnp.arange(NF, dtype=jnp.int32)[None, :]
    phase = (rows * freqs % NFFT).astype(jnp.float32) * (2.0 * math.pi / NFFT)
    return jnp.concatenate([jnp.cos(phase), -jnp.sin(phase)], axis=1).astype(jnp.bfloat16)

def lag_table(segments):
    freqs = jnp.arange(NF, dtype=jnp.int32)[:, None]
    shifts = jnp.arange(LAGS, dtype=jnp.int32)[None, :] - LAGS // 2
    phase = jnp.mod(freqs * shifts, NFFT).astype(jnp.float32) * (2.0 * math.pi / NFFT)
    weight = jnp.where(freqs == 0, 1.0, 2.0).astype(jnp.float32) / jnp.sqrt(jnp.float32(NFFT * segments))
    return jnp.concatenate([weight * jnp.cos(phase), -weight * jnp.sin(phase)], axis=0)

def whiten(spectrum):
    real_part = spectrum[..., :NF]
    imag_part = spectrum[..., NF:]
    power = real_part * real_part + imag_part * imag_part
    band_power = lax.optimization_barrier(jnp.mean(power.reshape(power.shape[:-1] + (NF // BAND, BAND)), axis=-1))
    factor = jnp.repeat(1.0 / jnp.sqrt(band_power + 1e-06), BAND, axis=-1)
    return jnp.concatenate([real_part * factor, imag_part * factor], axis=-1).astype(jnp.bfloat16)

def reference(samples, gap_start, gap_len, offsets):
    channels, total = samples.shape
    blocks = jnp.arange(total + HOP, dtype=jnp.int32) // BLK
    covered = jnp.any((blocks[None, None, :] >= gap_start[:, :, None]) & (blocks[None, None, :] < (gap_start + gap_len)[:, :, None]), axis=1)
    extended = jnp.concatenate([samples, jnp.zeros((channels, HOP), jnp.bfloat16)], axis=1)
    masked = jnp.where(covered, jnp.zeros_like(extended), extended)
    pieces = masked.reshape(channels, total // HOP + 1, HOP)
    frames = jnp.concatenate([pieces[:, :-1], pieces[:, 1:]], axis=2)
    taper = 0.5 - 0.5 * jnp.cos(jnp.arange(NFFT, dtype=jnp.int32).astype(jnp.float32) * (2.0 * math.pi / NFFT))
    tapered = (frames.astype(jnp.float32) * taper).astype(jnp.bfloat16)
    table = dft_table().astype(jnp.float32)
    grouped = tapered.reshape(channels // CH_DEV, CH_DEV, SEGMENTS, NFFT)

    def transform(group):
        spectrum = jnp.einsum('csn,nf->csf', group.astype(jnp.float32), table)
        return whiten(spectrum)
    whitened = lax.map(transform, grouped).reshape(channels, SEGMENTS, 2 * NF)
    padded = jnp.pad(whitened, ((R, R), (0, 0), (0, 0)))
    lags = lag_table(SEGMENTS)

    def one_slot(offset):
        partner = lax.dynamic_slice_in_dim(padded, (R + offset).astype(jnp.int32), channels, 0).astype(jnp.float32)
        own = whitened.astype(jnp.float32)
        real_own, imag_own = (own[..., :NF], own[..., NF:])
        real_far, imag_far = (partner[..., :NF], partner[..., NF:])
        real_sum = lax.optimization_barrier(jnp.sum(real_own * real_far + imag_own * imag_far, axis=1))
        imag_sum = lax.optimization_barrier(jnp.sum(imag_own * real_far - real_own * imag_far, axis=1))
        stack = jnp.concatenate([real_sum, imag_sum], axis=-1)
        return jnp.dot(stack, lags, precision=lax.Precision.HIGHEST, preferred_element_type=jnp.float32)
    return lax.map(one_slot, offsets)
```

```python
import math

import jax
import jax.numpy as jnp
import numpy as np
from jax import lax
from jax.experimental import pallas as pl
from jax.experimental.pallas import tpu as pltpu
from jax.sharding import PartitionSpec as P

NFFT = 2048
HALF = 1024
LAGS = 1024
BAND = 64
BLK = 256
LANE = 128


def transform_tables():
    rows = np.arange(HALF)[:, None]
    tabs = np.zeros((2, 2, HALF, 512), np.float32)
    for p in range(2):
        for jp in range(2):
            f = (2 * (256 * jp + np.arange(256)) + p)[None, :]
            phase = (rows * f % NFFT) * (2.0 * math.pi / NFFT)
            tabs[p, jp, :, :256] = np.cos(phase)
            tabs[p, jp, :, 256:] = -np.sin(phase)
    return tabs.astype(jnp.bfloat16)


def lag_table(segments):
    freqs = np.concatenate([np.arange(0, HALF, 2), np.arange(1, HALF, 2)])[:, None]
    shifts = np.arange(LAGS)[None, :] - LAGS // 2
    phase = (freqs * shifts % NFFT) * (2.0 * math.pi / NFFT)
    weight = np.where(freqs == 0, 1.0, 2.0) / math.sqrt(NFFT * segments)
    table = np.concatenate([weight * np.cos(phase), -weight * np.sin(phase)], axis=0)
    return table.astype(np.float32).astype(jnp.bfloat16)


def band_ones():
    place = np.arange(256) // 32
    return (place[:, None] == place[None, :]).astype(np.float32).astype(jnp.bfloat16)


def taper_row():
    n = np.arange(NFFT, dtype=np.float32)[None, :]
    return (0.5 - 0.5 * np.cos(n * np.float32(2.0 * math.pi / NFFT))).astype(np.float32)


def spectra(ext, place, taper, tabs, ones, even, odd, near, wide, diff):
    for s in range(16):
        low = ext[:, s * HALF : (s + 1) * HALF].astype(jnp.float32) * taper[:, :HALF]
        high = ext[:, (s + 1) * HALF : (s + 2) * HALF].astype(jnp.float32) * taper[:, HALF:]
        low = low.astype(jnp.bfloat16).astype(jnp.float32)
        high = high.astype(jnp.bfloat16).astype(jnp.float32)
        even[s * 32 : (s + 1) * 32, :] = (low + high).astype(jnp.bfloat16)
        odd[s * 32 : (s + 1) * 32, :] = (low - high).astype(jnp.bfloat16)

    @pl.loop(0, 4)
    def _(step):
        jp = step % 2
        part = step // 2
        rows = pl.ds(pl.multiple_of(part * 256, 256), 256)
        spec = [
            jnp.dot(half[rows, :], tabs[p, jp], preferred_element_type=jnp.float32)
            for p, half in enumerate((even, odd))
        ]
        power = sum(v[:, :256] * v[:, :256] + v[:, 256:] * v[:, 256:] for v in spec)
        total = jnp.dot(power.astype(jnp.bfloat16), ones[...], preferred_element_type=jnp.float32)
        factor = lax.rsqrt(total * (1.0 / BAND) + 1e-6)
        for p in range(2):
            c = (spec[p][:, :256] * factor).astype(jnp.bfloat16).astype(jnp.float32)
            d = (spec[p][:, 256:] * factor).astype(jnp.bfloat16).astype(jnp.float32)
            for dest, val in ((near, c), (wide, c + d), (diff, d - c)):
                for s in range(8):
                    for h in range(2):
                        dest[part * 8 + s, p * 4 + jp * 2 + h, place * 32 : (place + 1) * 32, :] = val[
                            s * 32 : (s + 1) * 32, h * LANE : (h + 1) * LANE
                        ]


def correlate(offs, first, slots, near, wide, diff, stack):
    @pl.loop(0, 32)
    def _(step):
        j = step // 4
        i = step % 4
        own = pl.ds(pl.multiple_of(32 + i * 8, 8), 8)
        far = [pl.ds(32 + i * 8 + offs[first + k], 8) for k in range(slots)]
        acc = [[None] * 3 for _ in range(slots)]
        for s in range(16):
            a = near[s, j, own, :]
            ab = wide[s, j, own, :]
            b = ab - a
            for k in range(slots):
                terms = (
                    near[s, j, far[k], :] * ab,
                    wide[s, j, far[k], :] * a,
                    diff[s, j, far[k], :] * b,
                )
                for t in range(3):
                    acc[k][t] = terms[t] if acc[k][t] is None else acc[k][t] + terms[t]
        col = pl.multiple_of(j * LANE, LANE)
        for k in range(slots):
            k1, k2, k3 = acc[k]
            rows = pl.ds(pl.multiple_of(k * 32 + i * 8, 8), 8)
            stack[rows, pl.ds(col, LANE)] = k1 + k3
            stack[rows, pl.ds(pl.multiple_of(col + HALF, LANE), LANE)] = k1 - k2


def kernel(slots, offs, low, mid, high, taper, tabs, lags, ones, out, even, odd, near, wide, diff, stack, stackb):
    for place, ext in enumerate((low, mid, high)):
        spectra(ext, place, taper, tabs, ones, even, odd, near, wide, diff)
    rows = slots * 32

    @pl.loop(0, 32 // slots)
    def _(block):
        correlate(offs, block * slots, slots, near, wide, diff, stack)
        stackb[...] = stack[...].astype(jnp.bfloat16)

        @pl.loop(0, LAGS // 256)
        def _(n):
            cols = pl.ds(pl.multiple_of(n * 256, 256), 256)
            fold = jnp.dot(stackb[...], lags[:, cols], preferred_element_type=jnp.float32)
            out[pl.ds(pl.multiple_of(block * rows, rows), rows), cols] = fold.astype(out.dtype)


def shards(samples, gap_start, gap_len, offsets, taper, tabs, lags, ones):
    channels, local_len = samples.shape
    tm_count = lax.axis_size("tm")
    chan_count = lax.axis_size("chan")
    slots = offsets.shape[0] // tm_count
    blocks = (lax.axis_index("tm") * local_len + jnp.arange(local_len, dtype=jnp.int32)) // BLK
    covered = jnp.any(
        (blocks[None, None, :] >= gap_start[:, :, None])
        & (blocks[None, None, :] < (gap_start + gap_len)[:, :, None]),
        axis=1,
    )
    masked = jnp.where(covered, jnp.zeros_like(samples), samples)
    back = [(i + 1, i) for i in range(tm_count - 1)]
    ext = jnp.concatenate([masked, lax.ppermute(masked[:, :HALF], "tm", back)], axis=1)
    forward = [(i, i + 1) for i in range(chan_count - 1)]
    low = lax.ppermute(ext, "chan", forward)
    high = lax.ppermute(ext, "chan", [(b, a) for a, b in forward])
    vmem = pl.BlockSpec(memory_space=pltpu.VMEM)
    part = pl.pallas_call(
        lambda *refs: kernel(slots, *refs),
        out_shape=jax.ShapeDtypeStruct((32 * channels, LAGS), jnp.bfloat16),
        in_specs=[pl.BlockSpec(memory_space=pltpu.SMEM)] + [vmem] * 7,
        out_specs=vmem,
        scratch_shapes=[
            pltpu.VMEM((512, HALF), jnp.bfloat16),
            pltpu.VMEM((512, HALF), jnp.bfloat16),
            pltpu.VMEM((16, 8, 96, LANE), jnp.float32),
            pltpu.VMEM((16, 8, 96, LANE), jnp.float32),
            pltpu.VMEM((16, 8, 96, LANE), jnp.float32),
            pltpu.VMEM((slots * 32, NFFT), jnp.float32),
            pltpu.VMEM((slots * 32, NFFT), jnp.bfloat16),
        ],
        compiler_params=pltpu.CompilerParams(vmem_limit_bytes=60 * 1024 * 1024),
    )(offsets, low, ext, high, taper, tabs, lags, ones)
    part = part.reshape(tm_count, slots, channels, LAGS)
    mixed = lax.all_to_all(part, "tm", split_axis=0, concat_axis=0)
    return jnp.sum(mixed.astype(jnp.float32), axis=0)


def solution(mesh):
    placed = (P(("win", "chan"), "tm"), P(("win", "chan"), None), P(("win", "chan"), None), P())
    inner = jax.shard_map(
        shards,
        mesh=mesh,
        in_specs=placed + (P(),) * 4,
        out_specs=P("tm", ("win", "chan"), None),
        check_vma=False,
    )

    def run(samples, gap_start, gap_len, offsets):
        segments = samples.shape[1] // HALF
        return inner(
            samples, gap_start, gap_len, offsets, taper_row(), transform_tables(), lag_table(segments), band_ones()
        )

    return run
```

```python
import math

import jax
import jax.numpy as jnp
import numpy as np
from jax import lax
from jax.experimental import pallas as pl
from jax.experimental.pallas import tpu as pltpu
from jax.sharding import PartitionSpec as P

NFFT = 2048
HALF = 1024
LAGS = 1024
BAND = 64
BLK = 256
LANE = 128


def transform_tables():
    rows = np.arange(HALF)[:, None]
    tabs = np.zeros((2, 2, HALF, 512), np.float32)
    for p in range(2):
        for jp in range(2):
            f = (2 * (256 * jp + np.arange(256)) + p)[None, :]
            phase = (rows * f % NFFT) * (2.0 * math.pi / NFFT)
            tabs[p, jp, :, :256] = np.cos(phase)
            tabs[p, jp, :, 256:] = -np.sin(phase)
    return tabs.astype(jnp.bfloat16)


def lag_table(segments):
    freqs = np.concatenate([np.arange(0, HALF, 2), np.arange(1, HALF, 2)])[:, None]
    shifts = np.arange(LAGS)[None, :] - LAGS // 2
    phase = (freqs * shifts % NFFT) * (2.0 * math.pi / NFFT)
    weight = np.where(freqs == 0, 1.0, 2.0) / math.sqrt(NFFT * segments)
    table = np.concatenate([weight * np.cos(phase), -weight * np.sin(phase)], axis=0)
    return table.astype(np.float32).astype(jnp.bfloat16)


def band_ones():
    place = np.arange(256) // 32
    return (place[:, None] == place[None, :]).astype(np.float32).astype(jnp.bfloat16)


def taper_row():
    n = np.arange(NFFT, dtype=np.float32)[None, :]
    return (0.5 - 0.5 * np.cos(n * np.float32(2.0 * math.pi / NFFT))).astype(np.float32)


def spectra(ext, place, taper, tabs, ones, even, odd, near, wide, diff):
    @pl.loop(0, 16)
    def _(s):
        begin = pl.multiple_of(s * HALF, HALF)
        low = ext[place, :, pl.ds(begin, HALF)].astype(jnp.float32) * taper[:, :HALF]
        high = ext[place, :, pl.ds(pl.multiple_of(begin + HALF, HALF), HALF)].astype(jnp.float32) * taper[:, HALF:]
        low = low.astype(jnp.bfloat16).astype(jnp.float32)
        high = high.astype(jnp.bfloat16).astype(jnp.float32)
        rows = pl.ds(pl.multiple_of(s * 32, 32), 32)
        even[rows, :] = (low + high).astype(jnp.bfloat16)
        odd[rows, :] = (low - high).astype(jnp.bfloat16)

    place_rows = pl.ds(pl.multiple_of(place * 32, 32), 32)

    @pl.loop(0, 4)
    def _(step):
        jp = step % 2
        part = step // 2
        rows = pl.ds(pl.multiple_of(part * 256, 256), 256)
        spec = [
            jnp.dot(half[rows, :], tabs[p, jp], preferred_element_type=jnp.float32)
            for p, half in enumerate((even, odd))
        ]
        power = sum(v[:, :256] * v[:, :256] + v[:, 256:] * v[:, 256:] for v in spec)
        total = jnp.dot(power.astype(jnp.bfloat16), ones[...], preferred_element_type=jnp.float32)
        factor = lax.rsqrt(total * (1.0 / BAND) + 1e-6)
        for p in range(2):
            c = (spec[p][:, :256] * factor).astype(jnp.bfloat16).astype(jnp.float32)
            d = (spec[p][:, 256:] * factor).astype(jnp.bfloat16).astype(jnp.float32)
            for dest, val in ((near, c), (wide, c + d), (diff, d - c)):
                for s in range(8):
                    for h in range(2):
                        dest[part * 8 + s, p * 4 + jp * 2 + h, place_rows, :] = val[
                            s * 32 : (s + 1) * 32, h * LANE : (h + 1) * LANE
                        ]


def correlate(offs, first, slots, near, wide, diff, stack):
    @pl.loop(0, 32)
    def _(step):
        j = step // 4
        i = step % 4
        own = pl.ds(pl.multiple_of(32 + i * 8, 8), 8)
        far = [pl.ds(32 + i * 8 + offs[first + k], 8) for k in range(slots)]
        acc = [[None] * 3 for _ in range(slots)]
        for s in range(16):
            a = near[s, j, own, :]
            ab = wide[s, j, own, :]
            b = ab - a
            for k in range(slots):
                terms = (
                    near[s, j, far[k], :] * ab,
                    wide[s, j, far[k], :] * a,
                    diff[s, j, far[k], :] * b,
                )
                for t in range(3):
                    acc[k][t] = terms[t] if acc[k][t] is None else acc[k][t] + terms[t]
        col = pl.multiple_of(j * LANE, LANE)
        for k in range(slots):
            k1, k2, k3 = acc[k]
            rows = pl.ds(pl.multiple_of(k * 32 + i * 8, 8), 8)
            stack[rows, pl.ds(col, LANE)] = k1 + k3
            stack[rows, pl.ds(pl.multiple_of(col + HALF, LANE), LANE)] = k1 - k2


MESH = pl.DeviceIdType.MESH


def kernel(
    slots, ranges, offs, starts, lens, x, taper, tabs, lags, ones, out,
    ext, even, odd, near, wide, diff, stack, stackb, sent, got,
    halo_send, halo_recv, sum_send, sum_recv,
):
    me, z = lax.axis_index("chan"), lax.axis_index("tm")
    win = lax.axis_index("win")
    chans = lax.axis_size("chan")
    local = x.shape[1]
    rows = slots * 32
    lower, upper = me > 0, me < chans - 1
    early, late = z > 0, z < ranges - 1

    barrier = pltpu.get_barrier_semaphore()
    for r in range(1, ranges):
        pl.semaphore_signal(
            barrier, inc=1, device_id=(win, me, lax.rem(z + r, ranges)), device_id_type=MESH
        )
    for side, there in ((-1, lower), (1, upper)):
        for dz, ahead in ((-1, early), (0, True), (1, late)):
            @pl.when(jnp.logical_and(there, ahead))
            def _(side=side, dz=dz):
                pl.semaphore_signal(
                    barrier, inc=1, device_id=(win, me + side, z + dz), device_id_type=MESH
                )

    @pl.loop(0, local // HALF)
    def _(s):
        begin = pl.multiple_of(s * HALF, HALF)
        for q in range(HALF // BLK):
            block = z * (local // BLK) + s * (HALF // BLK) + q
            cols = pl.ds(pl.multiple_of(begin + q * BLK, BLK), BLK)
            hit = (starts[...] <= block) & (block < starts[...] + lens[...])
            count = jnp.sum(hit.astype(jnp.float32), axis=1, keepdims=True)
            value = x[:, cols].astype(jnp.float32)
            ext[1, :, cols] = jnp.where(count > 0.0, 0.0, value).astype(jnp.bfloat16)

    edge = pl.ds(local, HALF)

    @pl.when(jnp.logical_not(late))
    def _():
        for p in range(3):
            ext[p, :, edge] = jnp.zeros((32, HALF), jnp.bfloat16)

    for p, there in ((0, lower), (2, upper)):
        @pl.when(jnp.logical_not(there))
        def _(p=p):
            @pl.loop(0, local // HALF)
            def _(s):
                ext[p, :, pl.ds(pl.multiple_of(s * HALF, HALF), HALF)] = jnp.zeros((32, HALF), jnp.bfloat16)

            @pl.when(late)
            def _():
                ext[p, :, edge] = jnp.zeros((32, HALF), jnp.bfloat16)

    sides = lower.astype(jnp.int32) + upper.astype(jnp.int32)
    around = 1 + early.astype(jnp.int32) + late.astype(jnp.int32)
    pl.semaphore_wait(barrier, ranges - 1 + sides * around)

    def body_copy(p, side):
        return pltpu.make_async_remote_copy(
            src_ref=ext.at[1, :, pl.ds(0, local)], dst_ref=ext.at[p, :, pl.ds(0, local)],
            send_sem=halo_send.at[2 * p], recv_sem=halo_recv.at[2 * p],
            device_id=(win, me + side, z), device_id_type=MESH,
        )

    def head_copy(p, side):
        return pltpu.make_async_remote_copy(
            src_ref=ext.at[1, :, pl.ds(0, HALF)], dst_ref=ext.at[p, :, edge],
            send_sem=halo_send.at[2 * p + 1], recv_sem=halo_recv.at[2 * p + 1],
            device_id=(win, me + side, z - 1), device_id_type=MESH,
        )

    @pl.when(early)
    def _():
        head_copy(1, 0).start()

    for p, side, there in ((0, 1, upper), (2, -1, lower)):
        @pl.when(there)
        def _(p=p, side=side):
            @pl.when(early)
            def _():
                head_copy(p, side).start()

            body_copy(p, side).start()

    @pl.loop(0, 3)
    def _(q):
        first = jnp.where(me % 2 == 0, 2, 0)
        place = jnp.where(q == 0, 1, jnp.where(q == 1, first, 2 - first))

        for p, there in ((0, lower), (1, None), (2, upper)):
            present = place == p if there is None else jnp.logical_and(place == p, there)

            @pl.when(present)
            def _(p=p):
                if p != 1:
                    body_copy(p, 0).wait_recv()

                @pl.when(late)
                def _():
                    head_copy(p, 0).wait_recv()

        spectra(ext, place, taper, tabs, ones, even, odd, near, wide, diff)

    def sum_copy(r):
        return pltpu.make_async_remote_copy(
            src_ref=sent.at[r - 1], dst_ref=got.at[r - 1],
            send_sem=sum_send.at[r - 1], recv_sem=sum_recv.at[r - 1],
            device_id=(win, me, lax.rem(z + r, ranges)), device_id_type=MESH,
        )

    @pl.loop(0, ranges)
    def _(t):
        r = ranges - 1 - t
        target = lax.rem(z + r, ranges)
        correlate(offs, target * slots, slots, near, wide, diff, stack)
        stackb[...] = stack[...].astype(jnp.bfloat16)

        @pl.loop(0, LAGS // 256)
        def _(n):
            cols = pl.ds(pl.multiple_of(n * 256, 256), 256)
            fold = jnp.dot(stackb[...], lags[:, cols], preferred_element_type=jnp.float32)

            @pl.when(r > 0)
            def _():
                sent[r - 1, :, cols] = fold.astype(jnp.bfloat16)

            @pl.when(r == 0)
            def _():
                out[:, cols] = fold

        @pl.when(r > 0)
        def _():
            sum_copy(r).start()

    @pl.loop(0, ranges - 1)
    def _(t):
        r = ranges - 1 - t
        sum_copy(r).wait_recv()

        @pl.loop(0, rows // 32)
        def _(n):
            part = pl.ds(pl.multiple_of(n * 32, 32), 32)
            out[part, :] = out[part, :] + got[r - 1, part, :].astype(jnp.float32)

    @pl.loop(0, ranges - 1)
    def _(t):
        sum_copy(ranges - 1 - t).wait_send()

    @pl.when(early)
    def _():
        head_copy(1, 0).wait_send()

    for p, side, there in ((0, 1, upper), (2, -1, lower)):
        @pl.when(there)
        def _(p=p, side=side):
            @pl.when(early)
            def _():
                head_copy(p, side).wait_send()

            body_copy(p, side).wait_send()


def shards(samples, gap_start, gap_len, offsets, taper, tabs, lags, ones):
    channels, local_len = samples.shape
    ranges = lax.axis_size("tm")
    slots = offsets.shape[0] // ranges
    rows = slots * channels
    vmem = pl.BlockSpec(memory_space=pltpu.VMEM)
    part = pl.pallas_call(
        lambda *refs: kernel(slots, ranges, *refs),
        out_shape=jax.ShapeDtypeStruct((rows, LAGS), jnp.float32),
        in_specs=[pl.BlockSpec(memory_space=pltpu.SMEM)] + [vmem] * 7,
        out_specs=vmem,
        scratch_shapes=[
            pltpu.VMEM((3, channels, local_len + HALF), jnp.bfloat16),
            pltpu.VMEM((512, HALF), jnp.bfloat16),
            pltpu.VMEM((512, HALF), jnp.bfloat16),
            pltpu.VMEM((16, 8, 96, LANE), jnp.float32),
            pltpu.VMEM((16, 8, 96, LANE), jnp.float32),
            pltpu.VMEM((16, 8, 96, LANE), jnp.float32),
            pltpu.VMEM((rows, NFFT), jnp.float32),
            pltpu.VMEM((rows, NFFT), jnp.bfloat16),
            pltpu.VMEM((ranges - 1, rows, LAGS), jnp.bfloat16),
            pltpu.VMEM((ranges - 1, rows, LAGS), jnp.bfloat16),
            pltpu.SemaphoreType.DMA((6,)),
            pltpu.SemaphoreType.DMA((6,)),
            pltpu.SemaphoreType.DMA((ranges - 1,)),
            pltpu.SemaphoreType.DMA((ranges - 1,)),
        ],
        compiler_params=pltpu.CompilerParams(
            vmem_limit_bytes=60 * 1024 * 1024, collective_id=0, has_side_effects=True
        ),
    )(offsets, gap_start, gap_len, samples, taper, tabs, lags, ones)
    return part.reshape(slots, channels, LAGS)


def solution(mesh):
    placed = (P(("win", "chan"), "tm"), P(("win", "chan"), None), P(("win", "chan"), None), P())
    inner = jax.shard_map(
        shards,
        mesh=mesh,
        in_specs=placed + (P(),) * 4,
        out_specs=P("tm", ("win", "chan"), None),
        check_vma=False,
    )

    def run(samples, gap_start, gap_len, offsets):
        segments = samples.shape[1] // HALF
        return inner(
            samples, gap_start, gap_len, offsets, taper_row(), transform_tables(), lag_table(segments), band_ones()
        )

    return run
```

```python
import math

import jax
import jax.numpy as jnp
import numpy as np
from jax import lax
from jax.experimental import pallas as pl
from jax.experimental.pallas import tpu as pltpu
from jax.sharding import PartitionSpec as P

NFFT = 2048
HALF = 1024
LAGS = 1024
BAND = 64
BLK = 256
LANE = 128


def transform_tables():
    rows = np.arange(HALF)[:, None]
    tabs = np.zeros((2, 2, HALF, 512), np.float32)
    for p in range(2):
        for jp in range(2):
            f = (2 * (256 * jp + np.arange(256)) + p)[None, :]
            phase = (rows * f % NFFT) * (2.0 * math.pi / NFFT)
            tabs[p, jp, :, :256] = np.cos(phase)
            tabs[p, jp, :, 256:] = -np.sin(phase)
    return tabs.astype(jnp.bfloat16)


def lag_table(segments):
    freqs = np.concatenate([np.arange(0, HALF, 2), np.arange(1, HALF, 2)])[:, None]
    shifts = np.arange(LAGS)[None, :] - LAGS // 2
    phase = (freqs * shifts % NFFT) * (2.0 * math.pi / NFFT)
    weight = np.where(freqs == 0, 1.0, 2.0) / math.sqrt(NFFT * segments)
    table = np.concatenate([weight * np.cos(phase), -weight * np.sin(phase)], axis=0)
    return table.astype(np.float32).astype(jnp.bfloat16)


def band_ones():
    place = np.arange(256) // 32
    return (place[:, None] == place[None, :]).astype(np.float32).astype(jnp.bfloat16)


def taper_row():
    n = np.arange(NFFT, dtype=np.float32)[None, :]
    return (0.5 - 0.5 * np.cos(n * np.float32(2.0 * math.pi / NFFT))).astype(np.float32)


def spectra(ext, place, taper, tabs, ones, even, odd, near, wide, diff):
    @pl.loop(0, 16)
    def _(s):
        begin = pl.multiple_of(s * HALF, HALF)
        low = ext[place, :, pl.ds(begin, HALF)].astype(jnp.float32) * taper[:, :HALF]
        high = ext[place, :, pl.ds(pl.multiple_of(begin + HALF, HALF), HALF)].astype(jnp.float32) * taper[:, HALF:]
        low = low.astype(jnp.bfloat16).astype(jnp.float32)
        high = high.astype(jnp.bfloat16).astype(jnp.float32)
        rows = pl.ds(pl.multiple_of(s * 32, 32), 32)
        even[rows, :] = (low + high).astype(jnp.bfloat16)
        odd[rows, :] = (low - high).astype(jnp.bfloat16)

    place_rows = pl.ds(pl.multiple_of(place * 32, 32), 32)

    @pl.loop(0, 4)
    def _(step):
        jp = step % 2
        part = step // 2
        rows = pl.ds(pl.multiple_of(part * 256, 256), 256)
        spec = [
            jnp.dot(half[rows, :], tabs[p, jp], preferred_element_type=jnp.float32)
            for p, half in enumerate((even, odd))
        ]
        power = sum(v[:, :256] * v[:, :256] + v[:, 256:] * v[:, 256:] for v in spec)
        total = jnp.dot(power.astype(jnp.bfloat16), ones[...], preferred_element_type=jnp.float32)
        factor = lax.rsqrt(total * (1.0 / BAND) + 1e-6)
        for p in range(2):
            c = (spec[p][:, :256] * factor).astype(jnp.bfloat16).astype(jnp.float32)
            d = (spec[p][:, 256:] * factor).astype(jnp.bfloat16).astype(jnp.float32)
            for dest, val in ((near, c), (wide, c + d), (diff, d - c)):
                for s in range(8):
                    for h in range(2):
                        dest[part * 8 + s, p * 4 + jp * 2 + h, place_rows, :] = val[
                            s * 32 : (s + 1) * 32, h * LANE : (h + 1) * LANE
                        ]


def correlate(offs, first, slots, near, wide, diff, stack):
    @pl.loop(0, 32)
    def _(step):
        j = step // 4
        i = step % 4
        own = pl.ds(pl.multiple_of(32 + i * 8, 8), 8)
        far = [pl.ds(32 + i * 8 + offs[first + k], 8) for k in range(slots)]
        acc = [[None] * 3 for _ in range(slots)]
        for s in range(16):
            a = near[s, j, own, :]
            ab = wide[s, j, own, :]
            b = ab - a
            for k in range(slots):
                terms = (
                    near[s, j, far[k], :] * ab,
                    wide[s, j, far[k], :] * a,
                    diff[s, j, far[k], :] * b,
                )
                for t in range(3):
                    acc[k][t] = terms[t] if acc[k][t] is None else acc[k][t] + terms[t]
        col = pl.multiple_of(j * LANE, LANE)
        for k in range(slots):
            k1, k2, k3 = acc[k]
            rows = pl.ds(pl.multiple_of(k * 32 + i * 8, 8), 8)
            stack[rows, pl.ds(col, LANE)] = k1 + k3
            stack[rows, pl.ds(pl.multiple_of(col + HALF, LANE), LANE)] = k1 - k2


MESH = pl.DeviceIdType.MESH


def kernel(
    slots, ranges, offs, starts, lens, x, taper, tabs_hbm, lags_hbm, ones, out,
    tabs, lags, ext, even, odd, near, wide, diff, stack, stackb, sent, got,
    table_sem, halo_send, halo_recv, sum_send, sum_recv,
):
    me, z = lax.axis_index("chan"), lax.axis_index("tm")
    win = lax.axis_index("win")
    chans = lax.axis_size("chan")
    local = x.shape[1]
    rows = slots * 32
    lower, upper = me > 0, me < chans - 1
    early, late = z > 0, z < ranges - 1

    load_tabs = pltpu.make_async_copy(tabs_hbm, tabs, table_sem.at[0])
    load_lags = pltpu.make_async_copy(lags_hbm, lags, table_sem.at[1])
    load_tabs.start()
    load_lags.start()
    barrier = pltpu.get_barrier_semaphore()
    for side, there in ((-1, lower), (0, True), (1, upper)):
        for dz, ahead in ((-1, early), (0, True), (1, late)):
            if side == 0 and dz == 0:
                continue

            @pl.when(jnp.logical_and(there, ahead))
            def _(side=side, dz=dz):
                pl.semaphore_signal(
                    barrier, inc=1, device_id=(win, me + side, z + dz), device_id_type=MESH
                )

    square = (32, 32)
    eye = (
        lax.broadcasted_iota(jnp.int32, square, 0) == lax.broadcasted_iota(jnp.int32, square, 1)
    ).astype(jnp.float32)

    def upright(value):
        return lax.dot_general(
            eye, value.astype(jnp.float32), (((1,), (1,)), ((), ())),
            precision=lax.Precision.HIGHEST, preferred_element_type=jnp.float32,
        )

    begins = upright(starts[...])
    ends = upright(starts[...] + lens[...])

    @pl.loop(0, local // HALF)
    def _(s):
        begin = pl.multiple_of(s * HALF, HALF)
        for q in range(HALF // BLK):
            block = (z * (local // BLK) + s * (HALF // BLK) + q).astype(jnp.float32)
            cols = pl.ds(pl.multiple_of(begin + q * BLK, BLK), BLK)
            hit = (begins <= block) & (block < ends)
            count = jnp.sum(hit.astype(jnp.float32), axis=1, keepdims=True)
            value = x[:, cols].astype(jnp.float32)
            ext[1, :, cols] = jnp.where(count > 0.0, 0.0, value).astype(jnp.bfloat16)

    edge = pl.ds(local, HALF)

    @pl.when(jnp.logical_not(late))
    def _():
        for p in range(3):
            ext[p, :, edge] = jnp.zeros((32, HALF), jnp.bfloat16)

    for p, there in ((0, lower), (2, upper)):
        @pl.when(jnp.logical_not(there))
        def _(p=p):
            @pl.loop(0, local // HALF)
            def _(s):
                ext[p, :, pl.ds(pl.multiple_of(s * HALF, HALF), HALF)] = jnp.zeros((32, HALF), jnp.bfloat16)

            @pl.when(late)
            def _():
                ext[p, :, edge] = jnp.zeros((32, HALF), jnp.bfloat16)

    sides = lower.astype(jnp.int32) + upper.astype(jnp.int32)
    around = 1 + early.astype(jnp.int32) + late.astype(jnp.int32)
    pl.semaphore_wait(barrier, (1 + sides) * around - 1)

    def body_copy(p, side):
        return pltpu.make_async_remote_copy(
            src_ref=ext.at[1, :, pl.ds(0, local)], dst_ref=ext.at[p, :, pl.ds(0, local)],
            send_sem=halo_send.at[2 * p], recv_sem=halo_recv.at[2 * p],
            device_id=(win, me + side, z), device_id_type=MESH,
        )

    def head_copy(p, side):
        return pltpu.make_async_remote_copy(
            src_ref=ext.at[1, :, pl.ds(0, HALF)], dst_ref=ext.at[p, :, edge],
            send_sem=halo_send.at[2 * p + 1], recv_sem=halo_recv.at[2 * p + 1],
            device_id=(win, me + side, z - 1), device_id_type=MESH,
        )

    @pl.when(early)
    def _():
        head_copy(1, 0).start()

    for p, side, there in ((0, 1, upper), (2, -1, lower)):
        @pl.when(there)
        def _(p=p, side=side):
            @pl.when(early)
            def _():
                head_copy(p, side).start()

            body_copy(p, side).start()

    load_tabs.wait()

    @pl.loop(0, 3)
    def _(q):
        first = jnp.where(me % 2 == 0, 2, 0)
        place = jnp.where(q == 0, 1, jnp.where(q == 1, first, 2 - first))

        for p, there in ((0, lower), (1, None), (2, upper)):
            present = place == p if there is None else jnp.logical_and(place == p, there)

            @pl.when(present)
            def _(p=p):
                if p != 1:
                    body_copy(p, 0).wait_recv()

                @pl.when(late)
                def _():
                    head_copy(p, 0).wait_recv()

        spectra(ext, place, taper, tabs, ones, even, odd, near, wide, diff)

    above, below = ranges - 1 - z, z
    most, least = jnp.maximum(above, below), jnp.minimum(above, below)
    far_side = jnp.where(above >= below, 1, -1)

    def target_of(t):
        u = jnp.maximum(t - (most - least), 0)
        alone = t < most - least
        away = jnp.where(alone, most - t, least - u // 2)
        side = jnp.where(jnp.logical_or(alone, u % 2 == 0), far_side, -far_side)
        return z + side * away

    def pass_copy(t, target):
        step = jnp.where(target > z, 1, -1)
        slot = jnp.where(jnp.logical_and(step < 0, target == z + step), ranges, target)
        return pltpu.make_async_remote_copy(
            src_ref=sent.at[t], dst_ref=got.at[slot],
            send_sem=sum_send.at[t], recv_sem=sum_recv.at[slot],
            device_id=(win, me, z + step), device_id_type=MESH,
        )

    def arrival(slot):
        return pltpu.make_async_remote_copy(
            src_ref=sent.at[0], dst_ref=got.at[slot],
            send_sem=sum_send.at[0], recv_sem=sum_recv.at[slot],
            device_id=(win, me, z), device_id_type=MESH,
        )

    def origin(target):
        return jnp.logical_or(
            jnp.logical_and(target > z, z == 0), jnp.logical_and(target < z, z == ranges - 1)
        )

    def forward(t):
        target = target_of(t)

        @pl.when(jnp.logical_not(origin(target)))
        def _():
            arrival(target).wait_recv()

            @pl.loop(0, rows // 32)
            def _(n):
                part = pl.ds(pl.multiple_of(n * 32, 32), 32)
                total = sent[t, part, :].astype(jnp.float32) + got[target, part, :].astype(jnp.float32)
                sent[t, part, :] = total.astype(jnp.bfloat16)

            pass_copy(t, target).start()

    @pl.loop(0, ranges)
    def _(t):
        target = target_of(t)
        last = t == ranges - 1
        correlate(offs, target * slots, slots, near, wide, diff, stack)
        stackb[...] = stack[...].astype(jnp.bfloat16)

        @pl.when(t == 0)
        def _():
            load_lags.wait()

        @pl.loop(0, LAGS // 256)
        def _(n):
            cols = pl.ds(pl.multiple_of(n * 256, 256), 256)
            fold = jnp.dot(stackb[...], lags[:, cols], preferred_element_type=jnp.float32)

            @pl.when(jnp.logical_not(last))
            def _():
                sent[t, :, cols] = fold.astype(jnp.bfloat16)

            @pl.when(last)
            def _():
                out[:, cols] = fold

        @pl.when(jnp.logical_and(jnp.logical_not(last), origin(target)))
        def _():
            pass_copy(t, target).start()

        @pl.when(jnp.logical_and(t >= 2, jnp.logical_not(last)))
        def _():
            forward(t - 2)

    for t in range(max(ranges - 3, 0), ranges - 1):
        forward(t)

    def finish(slot):
        arrival(slot).wait_recv()

        @pl.loop(0, rows // 32)
        def _(n):
            part = pl.ds(pl.multiple_of(n * 32, 32), 32)
            out[part, :] = out[part, :] + got[slot, part, :].astype(jnp.float32)

    @pl.when(early)
    def _():
        finish(z)

    @pl.when(late)
    def _():
        finish(ranges)

    @pl.loop(0, ranges - 1)
    def _(t):
        pass_copy(t, target_of(t)).wait_send()

    @pl.when(early)
    def _():
        head_copy(1, 0).wait_send()

    for p, side, there in ((0, 1, upper), (2, -1, lower)):
        @pl.when(there)
        def _(p=p, side=side):
            @pl.when(early)
            def _():
                head_copy(p, side).wait_send()

            body_copy(p, side).wait_send()


def shards(samples, gap_start, gap_len, offsets, taper, tabs, lags, ones):
    channels, local_len = samples.shape
    ranges = lax.axis_size("tm")
    slots = offsets.shape[0] // ranges
    rows = slots * channels
    vmem = pl.BlockSpec(memory_space=pltpu.VMEM)
    hbm = pl.BlockSpec(memory_space=pl.ANY)
    part = pl.pallas_call(
        lambda *refs: kernel(slots, ranges, *refs),
        out_shape=jax.ShapeDtypeStruct((rows, LAGS), jnp.float32),
        in_specs=[pl.BlockSpec(memory_space=pltpu.SMEM)] + [vmem] * 4 + [hbm] * 2 + [vmem],
        out_specs=vmem,
        scratch_shapes=[
            pltpu.VMEM(tabs.shape, jnp.bfloat16),
            pltpu.VMEM(lags.shape, jnp.bfloat16),
            pltpu.VMEM((3, channels, local_len + HALF), jnp.bfloat16),
            pltpu.VMEM((512, HALF), jnp.bfloat16),
            pltpu.VMEM((512, HALF), jnp.bfloat16),
            pltpu.VMEM((16, 8, 96, LANE), jnp.float32),
            pltpu.VMEM((16, 8, 96, LANE), jnp.float32),
            pltpu.VMEM((16, 8, 96, LANE), jnp.float32),
            pltpu.VMEM((rows, NFFT), jnp.float32),
            pltpu.VMEM((rows, NFFT), jnp.bfloat16),
            pltpu.VMEM((ranges - 1, rows, LAGS), jnp.bfloat16),
            pltpu.VMEM((ranges + 1, rows, LAGS), jnp.bfloat16),
            pltpu.SemaphoreType.DMA((2,)),
            pltpu.SemaphoreType.DMA((6,)),
            pltpu.SemaphoreType.DMA((6,)),
            pltpu.SemaphoreType.DMA((ranges - 1,)),
            pltpu.SemaphoreType.DMA((ranges + 1,)),
        ],
        compiler_params=pltpu.CompilerParams(
            vmem_limit_bytes=60 * 1024 * 1024, collective_id=0, has_side_effects=True
        ),
    )(offsets, gap_start.T, gap_len.T, samples, taper, tabs, lags, ones)
    return part.reshape(slots, channels, LAGS)


def solution(mesh):
    placed = (P(("win", "chan"), "tm"), P(("win", "chan"), None), P(("win", "chan"), None), P())
    inner = jax.shard_map(
        shards,
        mesh=mesh,
        in_specs=placed + (P(),) * 4,
        out_specs=P("tm", ("win", "chan"), None),
        check_vma=False,
    )

    def run(samples, gap_start, gap_len, offsets):
        segments = samples.shape[1] // HALF
        return inner(
            samples, gap_start, gap_len, offsets, taper_row(), transform_tables(), lag_table(segments), band_ones()
        )

    return run
```

```python
import math

import jax
import jax.numpy as jnp
import numpy as np
from jax import lax
from jax.experimental import pallas as pl
from jax.experimental.pallas import tpu as pltpu
from jax.sharding import PartitionSpec as P

NFFT = 2048
HALF = 1024
LAGS = 1024
BAND = 64
BLK = 256
LANE = 128
PITCH = 392


def transform_tables():
    rows = np.arange(HALF)[:, None]
    tabs = np.zeros((2, 2, HALF, 512), np.float32)
    for p in range(2):
        for jp in range(2):
            f = (2 * (256 * jp + np.arange(256)) + p)[None, :]
            phase = (rows * f % NFFT) * (2.0 * math.pi / NFFT)
            tabs[p, jp, :, :256] = np.cos(phase)
            tabs[p, jp, :, 256:] = -np.sin(phase)
    return tabs.astype(jnp.bfloat16)


def lag_table(segments):
    freqs = np.concatenate([np.arange(0, HALF, 2), np.arange(1, HALF, 2)])[:, None]
    shifts = np.arange(LAGS)[None, :] - LAGS // 2
    phase = (freqs * shifts % NFFT) * (2.0 * math.pi / NFFT)
    weight = np.where(freqs == 0, 1.0, 2.0) / math.sqrt(NFFT * segments)
    table = np.concatenate([weight * np.cos(phase), -weight * np.sin(phase)], axis=0)
    return table.astype(np.float32).astype(jnp.bfloat16)


def band_ones():
    place = np.arange(256) // 32
    return (place[:, None] == place[None, :]).astype(np.float32).astype(jnp.bfloat16)


def taper_row():
    n = np.arange(NFFT, dtype=np.float32)[None, :]
    return (0.5 - 0.5 * np.cos(n * np.float32(2.0 * math.pi / NFFT))).astype(np.float32)


def spectra(ext, place, taper, tabs, ones, even, odd, far):
    @pl.loop(0, 16)
    def _(s):
        begin = pl.multiple_of(s * HALF, HALF)
        low = ext[place, :, pl.ds(begin, HALF)].astype(jnp.float32) * taper[:, :HALF]
        high = ext[place, :, pl.ds(pl.multiple_of(begin + HALF, HALF), HALF)].astype(jnp.float32) * taper[:, HALF:]
        low = low.astype(jnp.bfloat16).astype(jnp.float32)
        high = high.astype(jnp.bfloat16).astype(jnp.float32)
        rows = pl.ds(pl.multiple_of(s * 32, 32), 32)
        even[rows, :] = (low + high).astype(jnp.bfloat16)
        odd[rows, :] = (low - high).astype(jnp.bfloat16)

    @pl.loop(0, 4)
    def _(step):
        jp = step % 2
        part = step // 2
        rows = pl.ds(pl.multiple_of(part * 256, 256), 256)
        spec = [
            jnp.dot(half[rows, :], tabs[p, jp], preferred_element_type=jnp.float32)
            for p, half in enumerate((even, odd))
        ]
        power = sum(v[:, :256] * v[:, :256] + v[:, 256:] * v[:, 256:] for v in spec)
        total = jnp.dot(power.astype(jnp.bfloat16), ones[...], preferred_element_type=jnp.float32)
        factor = lax.rsqrt(total * (1.0 / BAND) + 1e-6)
        for p in range(2):
            c = (spec[p][:, :256] * factor).astype(jnp.bfloat16).astype(jnp.float32)
            d = (spec[p][:, 256:] * factor).astype(jnp.bfloat16).astype(jnp.float32)
            for t, val in enumerate((c, c + d, d - c)):
                for s in range(8):
                    for h in range(2):
                        for g in range(4):
                            row = (place * 32 + g * 8) * PITCH + (part * 8 + s) * 24 + t * 8 + p * 4 + jp * 2 + h
                            far[pl.ds(row, 8, stride=PITCH), :] = val[
                                s * 32 + g * 8 : s * 32 + g * 8 + 8, h * LANE : (h + 1) * LANE
                            ]


def correlate(offs, first, slots, far, stack, pitch):
    @pl.loop(0, 32)
    def _(c):
        own = pl.multiple_of((32 + c) * PITCH, 8)
        base = [(32 + c + offs[first + k]) * PITCH for k in range(slots)]
        acc = [[None] * 3 for _ in range(slots)]
        for s in range(16):
            a = far[pl.ds(own + s * 24, 8), :]
            ab = far[pl.ds(own + s * 24 + 8, 8), :]
            b = ab - a
            for k in range(slots):
                terms = (
                    far[pl.ds(base[k] + s * 24, 8), :] * ab,
                    far[pl.ds(base[k] + s * 24 + 8, 8), :] * a,
                    far[pl.ds(base[k] + s * 24 + 16, 8), :] * b,
                )
                for t in range(3):
                    acc[k][t] = terms[t] if acc[k][t] is None else acc[k][t] + terms[t]
        for k in range(slots):
            k1, k2, k3 = acc[k]
            stack[pl.ds(k * 32 + c, 8, stride=pitch), :] = k1 + k3
            stack[pl.ds(8 * pitch + k * 32 + c, 8, stride=pitch), :] = k1 - k2


MESH = pl.DeviceIdType.MESH


def kernel(
    slots, ranges, offs, starts, lens, x, taper, tabs_hbm, lags_hbm, ones, out,
    tabs, lags, ext, even, odd, far, stack, stackb, sent, got,
    table_sem, halo_send, halo_recv, sum_send, sum_recv,
):
    me, z = lax.axis_index("chan"), lax.axis_index("tm")
    win = lax.axis_index("win")
    chans = lax.axis_size("chan")
    local = x.shape[1]
    rows = slots * 32
    lower, upper = me > 0, me < chans - 1
    early, late = z > 0, z < ranges - 1

    load_tabs = pltpu.make_async_copy(tabs_hbm, tabs, table_sem.at[0])
    load_lags = pltpu.make_async_copy(lags_hbm, lags, table_sem.at[1])
    load_tabs.start()
    load_lags.start()
    barrier = pltpu.get_barrier_semaphore()
    for side, there in ((-1, lower), (0, True), (1, upper)):
        for dz, ahead in ((-1, early), (0, True), (1, late)):
            if side == 0 and dz == 0:
                continue

            @pl.when(jnp.logical_and(there, ahead))
            def _(side=side, dz=dz):
                pl.semaphore_signal(
                    barrier, inc=1, device_id=(win, me + side, z + dz), device_id_type=MESH
                )

    square = (32, 32)
    eye = (
        lax.broadcasted_iota(jnp.int32, square, 0) == lax.broadcasted_iota(jnp.int32, square, 1)
    ).astype(jnp.float32)

    def upright(value):
        return lax.dot_general(
            eye, value.astype(jnp.float32), (((1,), (1,)), ((), ())),
            precision=lax.Precision.HIGHEST, preferred_element_type=jnp.float32,
        )

    begins = upright(starts[...])
    ends = upright(starts[...] + lens[...])

    @pl.loop(0, local // HALF)
    def _(s):
        begin = pl.multiple_of(s * HALF, HALF)
        for q in range(HALF // BLK):
            block = (z * (local // BLK) + s * (HALF // BLK) + q).astype(jnp.float32)
            cols = pl.ds(pl.multiple_of(begin + q * BLK, BLK), BLK)
            hit = (begins <= block) & (block < ends)
            count = jnp.sum(hit.astype(jnp.float32), axis=1, keepdims=True)
            value = x[:, cols].astype(jnp.float32)
            ext[1, :, cols] = jnp.where(count > 0.0, 0.0, value).astype(jnp.bfloat16)

    edge = pl.ds(local, HALF)

    @pl.when(jnp.logical_not(late))
    def _():
        for p in range(3):
            ext[p, :, edge] = jnp.zeros((32, HALF), jnp.bfloat16)

    for p, there in ((0, lower), (2, upper)):
        @pl.when(jnp.logical_not(there))
        def _(p=p):
            @pl.loop(0, local // HALF)
            def _(s):
                ext[p, :, pl.ds(pl.multiple_of(s * HALF, HALF), HALF)] = jnp.zeros((32, HALF), jnp.bfloat16)

            @pl.when(late)
            def _():
                ext[p, :, edge] = jnp.zeros((32, HALF), jnp.bfloat16)

    sides = lower.astype(jnp.int32) + upper.astype(jnp.int32)
    around = 1 + early.astype(jnp.int32) + late.astype(jnp.int32)
    pl.semaphore_wait(barrier, (1 + sides) * around - 1)

    def body_copy(p, side):
        return pltpu.make_async_remote_copy(
            src_ref=ext.at[1, :, pl.ds(0, local)], dst_ref=ext.at[p, :, pl.ds(0, local)],
            send_sem=halo_send.at[2 * p], recv_sem=halo_recv.at[2 * p],
            device_id=(win, me + side, z), device_id_type=MESH,
        )

    def head_copy(p, side):
        return pltpu.make_async_remote_copy(
            src_ref=ext.at[1, :, pl.ds(0, HALF)], dst_ref=ext.at[p, :, edge],
            send_sem=halo_send.at[2 * p + 1], recv_sem=halo_recv.at[2 * p + 1],
            device_id=(win, me + side, z - 1), device_id_type=MESH,
        )

    @pl.when(early)
    def _():
        head_copy(1, 0).start()

    for p, side, there in ((0, 1, upper), (2, -1, lower)):
        @pl.when(there)
        def _(p=p, side=side):
            @pl.when(early)
            def _():
                head_copy(p, side).start()

            body_copy(p, side).start()

    load_tabs.wait()

    @pl.loop(0, 3)
    def _(q):
        first = jnp.where(me % 2 == 0, 2, 0)
        place = jnp.where(q == 0, 1, jnp.where(q == 1, first, 2 - first))

        for p, there in ((0, lower), (1, None), (2, upper)):
            present = place == p if there is None else jnp.logical_and(place == p, there)

            @pl.when(present)
            def _(p=p):
                if p != 1:
                    body_copy(p, 0).wait_recv()

                @pl.when(late)
                def _():
                    head_copy(p, 0).wait_recv()

        spectra(ext, place, taper, tabs, ones, even, odd, far)

    above, below = ranges - 1 - z, z
    most, least = jnp.maximum(above, below), jnp.minimum(above, below)
    far_side = jnp.where(above >= below, 1, -1)

    def target_of(t):
        u = jnp.maximum(t - (most - least), 0)
        alone = t < most - least
        away = jnp.where(alone, most - t, least - u // 2)
        side = jnp.where(jnp.logical_or(alone, u % 2 == 0), far_side, -far_side)
        return z + side * away

    def pass_copy(t, target):
        step = jnp.where(target > z, 1, -1)
        slot = jnp.where(jnp.logical_and(step < 0, target == z + step), ranges, target)
        return pltpu.make_async_remote_copy(
            src_ref=sent.at[t], dst_ref=got.at[slot],
            send_sem=sum_send.at[t], recv_sem=sum_recv.at[slot],
            device_id=(win, me, z + step), device_id_type=MESH,
        )

    def arrival(slot):
        return pltpu.make_async_remote_copy(
            src_ref=sent.at[0], dst_ref=got.at[slot],
            send_sem=sum_send.at[0], recv_sem=sum_recv.at[slot],
            device_id=(win, me, z), device_id_type=MESH,
        )

    def origin(target):
        return jnp.logical_or(
            jnp.logical_and(target > z, z == 0), jnp.logical_and(target < z, z == ranges - 1)
        )

    def forward(t):
        target = target_of(t)

        @pl.when(jnp.logical_not(origin(target)))
        def _():
            arrival(target).wait_recv()

            @pl.loop(0, rows // 32)
            def _(n):
                part = pl.ds(pl.multiple_of(n * 32, 32), 32)
                total = sent[t, part, :].astype(jnp.float32) + got[target, part, :].astype(jnp.float32)
                sent[t, part, :] = total.astype(jnp.bfloat16)

            pass_copy(t, target).start()

    @pl.loop(0, ranges)
    def _(t):
        target = target_of(t)
        last = t == ranges - 1
        correlate(offs, target * slots, slots, far, stack, rows + 8)
        for j in range(16):
            block = stack[pl.ds(j * (rows + 8), rows), :]
            stackb[:, j * LANE : (j + 1) * LANE] = block.astype(jnp.bfloat16)

        @pl.when(t == 0)
        def _():
            load_lags.wait()

        @pl.loop(0, LAGS // 256)
        def _(n):
            cols = pl.ds(pl.multiple_of(n * 256, 256), 256)
            fold = jnp.dot(stackb[...], lags[:, cols], preferred_element_type=jnp.float32)

            @pl.when(jnp.logical_not(last))
            def _():
                sent[t, :, cols] = fold.astype(jnp.bfloat16)

            @pl.when(last)
            def _():
                out[:, cols] = fold

        @pl.when(jnp.logical_and(jnp.logical_not(last), origin(target)))
        def _():
            pass_copy(t, target).start()

        @pl.when(jnp.logical_and(t >= 2, jnp.logical_not(last)))
        def _():
            forward(t - 2)

    for t in range(max(ranges - 3, 0), ranges - 1):
        forward(t)

    def finish(slot):
        arrival(slot).wait_recv()

        @pl.loop(0, rows // 32)
        def _(n):
            part = pl.ds(pl.multiple_of(n * 32, 32), 32)
            out[part, :] = out[part, :] + got[slot, part, :].astype(jnp.float32)

    @pl.when(early)
    def _():
        finish(z)

    @pl.when(late)
    def _():
        finish(ranges)

    @pl.loop(0, ranges - 1)
    def _(t):
        pass_copy(t, target_of(t)).wait_send()

    @pl.when(early)
    def _():
        head_copy(1, 0).wait_send()

    for p, side, there in ((0, 1, upper), (2, -1, lower)):
        @pl.when(there)
        def _(p=p, side=side):
            @pl.when(early)
            def _():
                head_copy(p, side).wait_send()

            body_copy(p, side).wait_send()


def shards(samples, gap_start, gap_len, offsets, taper, tabs, lags, ones):
    channels, local_len = samples.shape
    ranges = lax.axis_size("tm")
    slots = offsets.shape[0] // ranges
    rows = slots * channels
    vmem = pl.BlockSpec(memory_space=pltpu.VMEM)
    hbm = pl.BlockSpec(memory_space=pl.ANY)
    part = pl.pallas_call(
        lambda *refs: kernel(slots, ranges, *refs),
        out_shape=jax.ShapeDtypeStruct((rows, LAGS), jnp.float32),
        in_specs=[pl.BlockSpec(memory_space=pltpu.SMEM)] + [vmem] * 4 + [hbm] * 2 + [vmem],
        out_specs=vmem,
        scratch_shapes=[
            pltpu.VMEM(tabs.shape, jnp.bfloat16),
            pltpu.VMEM(lags.shape, jnp.bfloat16),
            pltpu.VMEM((3, channels, local_len + HALF), jnp.bfloat16),
            pltpu.VMEM((512, HALF), jnp.bfloat16),
            pltpu.VMEM((512, HALF), jnp.bfloat16),
            pltpu.VMEM((96 * PITCH, LANE), jnp.float32),
            pltpu.VMEM((16 * (rows + 8), LANE), jnp.float32),
            pltpu.VMEM((rows, NFFT), jnp.bfloat16),
            pltpu.VMEM((ranges - 1, rows, LAGS), jnp.bfloat16),
            pltpu.VMEM((ranges + 1, rows, LAGS), jnp.bfloat16),
            pltpu.SemaphoreType.DMA((2,)),
            pltpu.SemaphoreType.DMA((6,)),
            pltpu.SemaphoreType.DMA((6,)),
            pltpu.SemaphoreType.DMA((ranges - 1,)),
            pltpu.SemaphoreType.DMA((ranges + 1,)),
        ],
        compiler_params=pltpu.CompilerParams(
            vmem_limit_bytes=60 * 1024 * 1024, collective_id=0, has_side_effects=True
        ),
    )(offsets, gap_start.T, gap_len.T, samples, taper, tabs, lags, ones)
    return part.reshape(slots, channels, LAGS)


def solution(mesh):
    placed = (P(("win", "chan"), "tm"), P(("win", "chan"), None), P(("win", "chan"), None), P())
    inner = jax.shard_map(
        shards,
        mesh=mesh,
        in_specs=placed + (P(),) * 4,
        out_specs=P("tm", ("win", "chan"), None),
        check_vma=False,
    )

    def run(samples, gap_start, gap_len, offsets):
        segments = samples.shape[1] // HALF
        return inner(
            samples, gap_start, gap_len, offsets, taper_row(), transform_tables(), lag_table(segments), band_ones()
        )

    return run
```
